512 devices in a mesh: row: 32 (over x, y), col: 16 (over z, core).
Axes of the slice: x: 4, y: 8, z: 8, core: 2. Of those that a mesh axis runs over, the one named last changes fastest.
Arguments:
- hessian: float32 [2, 8192, 4, 4096], P(None, 'row', None, 'col'), as said below
Outputs:
- factored: float32 [2, 8192, 4, 4096], P(None, 'row', None, 'col')
Inputs may be any that keep to these rules, and one draw needn't show every extreme that they name: hessian, read as the 16384 x 16384 matrix H0, is symmetric and positive definite.
All inputs are finite; a program needn't handle non-finite values.
Results may differ from the reference program's by a relative error of at most 0.0003.
Values sent between devices are 32-bit elements; how exact they have to be, the bound alone decides.
A program may use at most 64 MiB of HBM per device.

```python
import jax
import jax.numpy as jnp
from jax import lax

N = 16384
BLOCK = 256
SAMPLES = 1024
RCYC = 2
CCYC = 4


def draw_hessian(key, part):
    base = jax.random.fold_in(key, 7)
    key_scale, key_data, key_damp = jax.random.split(base, 3)
    scales = jnp.exp(jax.random.uniform(key_scale, (N, 1), jnp.float32, jnp.log(0.3), jnp.log(3.0)))
    samples = jax.random.normal(key_data, (N, SAMPLES), jnp.float32) * scales
    gram = jnp.dot(samples, samples.T, precision=lax.Precision.HIGHEST) / SAMPLES
    damping = jax.random.uniform(key_damp, (N,), jnp.float32, 0.05, 0.5) * scales[:, 0] * scales[:, 0]
    places = jnp.arange(N, dtype=jnp.int32)
    gram = gram.at[places, places].add(damping)
    return gram.reshape(RCYC, N // RCYC, CCYC, N // CCYC)


def setup_inputs(seed: int = 0) -> dict:
    seeds = jax.random.split(jax.random.key(seed), 2)
    return {
        "hessian": draw_hessian(jax.random.fold_in(seeds[1], 71), 0),
    }


def reference(hessian):
    matrix = hessian.reshape(N, N)
    identity = jnp.eye(BLOCK, dtype=matrix.dtype)
    positions = jnp.arange(N, dtype=jnp.int32)
    offsets = jnp.arange(BLOCK, dtype=jnp.int32)
    panels = []
    for panel_index in range(2):
        start = panel_index * BLOCK
        diagonal = matrix[start:start + BLOCK, start:start + BLOCK]
        lower_factor = jnp.linalg.cholesky(diagonal)
        inverse = lax.linalg.triangular_solve(lower_factor, identity, left_side=True, lower=True)
        own_panel = jnp.dot(matrix[:, start:start + BLOCK], inverse.T, precision=lax.Precision.HIGHEST)
        keep_mask = positions[:, None] >= start + offsets[None, :]
        own_panel = jnp.where(keep_mask, own_panel, jnp.zeros_like(own_panel))
        matrix = matrix - jnp.dot(own_panel, own_panel.T, precision=lax.Precision.HIGHEST)
        panels.append(own_panel)
    result = matrix.at[:2 * BLOCK, 2 * BLOCK:].set(0.0)
    result = result.at[:, :2 * BLOCK].set(jnp.concatenate(panels, axis=1))
    return result.reshape(RCYC, N // RCYC, CCYC, N // CCYC)
```

```python
import functools

import jax
import jax.numpy as jnp
from jax import lax
from jax.experimental import pallas as pl
from jax.experimental.pallas import tpu as pltpu
from jax.sharding import PartitionSpec as P

F = jnp.float32
HI = lax.Precision.HIGHEST
MESH = pl.DeviceIdType.MESH
W = 256


def recip(p):
    r = pl.reciprocal(p, approx=True)
    return r * (2.0 - p * r)

def leaf(m):
    m = list(m)
    sub = lax.broadcasted_iota(jnp.int32, (8, 128), 0)
    out = []
    for g in range(8):
        c = [[jnp.broadcast_to(m[v][:, 64 + 8 * g + k:65 + 8 * g + k], (8, 128)) for v in range(g, 8)] for k in range(8)]
        top = m[g]
        pivots = jnp.ones((8, 128), F)
        scaled_rows = []
        for k in range(8):
            col = c[k]
            pivot = jnp.broadcast_to(col[0][k:k + 1, :], (8, 128))
            r = recip(pivot)
            row = jnp.broadcast_to(top[k:k + 1, :], (8, 128)) * r
            scaled_rows.append(row)
            pivots = jnp.where(sub == k, pivot, pivots)
            top = top - jnp.where(sub > k, col[0], 0.0) * row
            for n in range(k + 1, 8):
                s = jnp.broadcast_to(col[0][n:n + 1, :], (8, 128)) * r
                c[n] = [a - b * s for a, b in zip(c[n], col)]
        for v in range(g + 1, 8):
            acc = m[v]
            for k in range(8):
                acc = acc - c[k][v - g] * scaled_rows[k]
            m[v] = acc
        out.append(top * lax.rsqrt(pivots))
    return out

class Comm:
    def __init__(self, nx, ny, nz, h, hv, rsrc, cbuf, rbuf, vbuf, dbuf, sems):
        self.nx, self.ny, self.nz = nx, ny, nz
        self.h, self.hv, self.rsrc, self.cbuf, self.rbuf = h, hv, rsrc, cbuf, rbuf
        self.vbuf, self.dbuf = vbuf, dbuf
        self.sems = sems
        self.row = lax.axis_index("row")
        self.col = lax.axis_index("col")
        self.x, self.y = self.row // ny, self.row % ny
        self.z, self.k = self.col // 2, self.col % 2
        self.root = jnp.logical_and(self.row == 0, self.col == 0)

    def at(self, x=None, y=None, z=None, k=None):
        x = self.x if x is None else x
        y = self.y if y is None else y
        z = self.z if z is None else z
        k = self.k if k is None else k
        return (x * self.ny + y, z * 2 + k)

    def barrier(self):
        nx, ny, nz = self.nx, self.ny, self.nz
        sem = pltpu.get_barrier_semaphore()

        def tell(device):
            pl.semaphore_signal(sem, inc=1, device_id=device, device_id_type=MESH)

        for root in range(2):
            pl.when(self.row != root)(lambda root=root: tell((root, self.col)))
        pl.when(self.z != 0)(lambda: tell(self.at(z=0)))
        tell(self.at(k=1 - self.k))
        for d in (1, -1):
            tell(self.at(y=(self.y + d) % ny))
            tell(self.at(z=(self.z + d) % nz))
        for d in range(1, nx):
            tell(self.at(x=(self.x + d) % nx))
        pl.when(self.root)(lambda: tell((1, 1)))
        total = 5 + nx - 1
        total = total + jnp.where(self.row < 2, nx * ny - 1, 0) + jnp.where(self.z == 0, nz - 1, 0)
        total = total + jnp.where(self.d_source(1), 1, 0)
        pl.semaphore_wait(sem, total)

    def remote(self, src, dst, send, recv, device):
        return pltpu.make_async_remote_copy(
            src_ref=src, dst_ref=dst, send_sem=send, recv_sem=recv, device_id=device, device_id_type=MESH
        )

    def scatter_c(self):
        nx, ny = self.nx, self.ny
        n = nx * ny
        sems_s, sems_r, local = self.sems["cs_send"], self.sems["cs_recv"], self.sems["local"]
        size = self.cbuf.shape[3]
        for root in range(2):

            @pl.when(self.row == root)
            def _(root=root):
                def send(i, carry):
                    p = (i % nx) * ny + (i // nx + root) % ny
                    copy = self.remote(
                        self.h.at[pl.ds(p * size, size)],
                        self.cbuf.at[root, p // ny, p % ny],
                        sems_s.at[p], sems_r.at[root], (p, self.col),
                    )
                    pl.when(p != root)(copy.start)
                    return carry
                lax.fori_loop(0, n, send, 0)
                pltpu.make_async_copy(
                    self.h.at[pl.ds(root * size, size)], self.cbuf.at[root, 0, root], local.at[root]
                ).start()

    def scatter_c_wait(self, root):
        size = self.cbuf.shape[3]

        @pl.when(self.row == root)
        def _():
            pltpu.make_async_copy(
                self.h.at[pl.ds(root * size, size)], self.cbuf.at[root, 0, root], self.sems["local"].at[root]
            ).wait()

        @pl.when(self.row != root)
        def _():
            piece = self.cbuf.at[root, self.x, self.y]
            self.remote(piece, piece, self.sems["cs_send"].at[0], self.sems["cs_recv"].at[root], self.at()).wait_recv()

    def scatter_c_done(self):
        size = self.cbuf.shape[3]
        for root in range(2):

            @pl.when(self.row == root)
            def _(root=root):
                def done(p, carry):
                    copy = self.remote(
                        self.h.at[pl.ds(p * size, size)], self.cbuf.at[root, p // self.ny, p % self.ny],
                        self.sems["cs_send"].at[p], self.sems["cs_recv"].at[root], (p, self.col),
                    )
                    pl.when(p != root)(copy.wait_send)
                    return carry
                lax.fori_loop(0, self.nx * self.ny, done, 0)

    def scatter_r_copy(self, q):
        return self.remote(
            self.rsrc.at[q], self.rbuf.at[self.k, q], self.sems["rs_send"].at[q], self.sems["rs_recv"], self.at(z=q)
        )

    def scatter_r_local(self):
        return [
            pltpu.make_async_copy(self.rsrc.at[0], self.rbuf.at[kk, 0], self.sems["local"].at[2]) for kk in range(2)
        ]

    def scatter_r(self):
        @pl.when(self.z == 0)
        def _():
            for q in range(1, self.nz):
                self.scatter_r_copy(q).start()
            for kk in range(2):
                pl.when(self.k == kk)(self.scatter_r_local()[kk].start)

    def scatter_r_wait(self):
        @pl.when(self.z == 0)
        def _():
            for kk in range(2):
                pl.when(self.k == kk)(self.scatter_r_local()[kk].wait)

        @pl.when(self.z != 0)
        def _():
            piece = self.rbuf.at[self.k, self.z]
            self.remote(piece, piece, self.sems["rs_send"].at[0], self.sems["rs_recv"], self.at()).wait_recv()

    def scatter_r_done(self):
        @pl.when(self.z == 0)
        def _():
            for q in range(1, self.nz):
                self.scatter_r_copy(q).wait_send()

    def ring(self, name, n, me, device, piece, step):
        half = n // 2
        out = []
        for way, sign in enumerate((1, -1)):
            index = (me - sign * (step - 1)) % n
            ref = piece(index, way if step == half else None)
            send = self.sems[name].at[0, way, step - 1]
            recv = self.sems[name].at[1, way, step - 1]
            out.append(self.remote(ref, ref, send, recv, device((me + sign) % n)))
        return out

    def ring_start(self, name, *args):
        for copy in self.ring(name, *args):
            copy.start()

    def ring_wait(self, name, n, me, device, piece, step):
        half = n // 2
        for way, sign in enumerate((1, -1)):
            index = (me - sign * step) % n
            ref = piece(index, way if step == half else None)
            send = self.sems[name].at[0, way, step - 1]
            recv = self.sems[name].at[1, way, step - 1]
            self.remote(ref, ref, send, recv, device((me + sign) % n)).wait_recv()

    def ring_done(self, name, *args):
        for copy in self.ring(name, *args):
            copy.wait_send()

    def rings(self):
        c = self.cbuf
        hs = c.shape[3] // 2
        hr = self.rbuf.shape[3] // 2

        def px0(i, h):
            ref = c.at[0, i, self.y]
            return ref if h is None else ref.at[pl.ds(h * hs, hs)]

        def py0(i, h):
            if h is None:
                return c.at[0, :, i]
            return c.at[0, :, i, pl.ds(h * hs, hs)]

        def py1(i, h):
            ref = c.at[1, self.x, i]
            return ref if h is None else ref.at[pl.ds(h * hs, hs)]

        def px1(i, h):
            if h is None:
                return c.at[1, i]
            return c.at[1, i, pl.ds(h * (self.ny // 2), self.ny // 2)]

        def pz(i, h):
            if h is None:
                return self.rbuf.at[self.k, i]
            return self.rbuf.at[self.k, i, h]

        dx = lambda i: self.at(x=i)
        dy = lambda i: self.at(y=i)
        dz = lambda i: self.at(z=i)
        return {
            "x0": ("x0", self.nx, self.x, dx, px0),
            "y0": ("y0", self.ny, self.y, dy, py0),
            "y1": ("y1", self.ny, self.y, dy, py1),
            "x1": ("x1", self.nx, self.x, dx, px1),
            "z": ("z", self.nz, self.z, dz, pz),
        }

    def swap_copy(self, kk):
        return self.remote(
            self.rbuf.at[kk], self.rbuf.at[kk], self.sems["swap"].at[0], self.sems["swap"].at[1], self.at(k=1 - self.k)
        )

    def swap_start(self):
        for kk in range(2):
            pl.when(self.k == kk)(self.swap_copy(kk).start)

    def swap_wait(self):
        for kk in range(2):
            pl.when(self.k != kk)(self.swap_copy(kk).wait_recv)

    def swap_done(self):
        for kk in range(2):
            pl.when(self.k == kk)(self.swap_copy(kk).wait_send)

    def prepare(self):
        @pl.when(self.z == 0)
        def _():
            nq, _, size, _ = self.rsrc.shape
            for q in range(nq):
                for ct in range(2):
                    self.rsrc[q, ct] = self.hv[pl.ds(q * size * 8 + ct * 4, size, stride=8), :]

    def d_source(self, b):
        return jnp.logical_and(self.row == b, self.col == 1)

    def d_copy(self, b):
        return self.remote(
            self.rsrc.at[pl.ds(0, self.dbuf.shape[1])], self.dbuf.at[b], self.sems["d"].at[0], self.sems["d"].at[1 + b], (0, 0)
        )

    def d_send(self):
        for b in range(2):
            pl.when(self.d_source(b))(lambda b=b: self.d_copy(b).start())

    def d_done(self):
        for b in range(2):
            pl.when(self.d_source(b))(lambda b=b: self.d_copy(b).wait_send())

    def v_stages(self, j):
        chunk = self.vbuf.at[j, 0] if j < 4 else self.vbuf.at[j]
        send, recv = self.sems["v_send"], self.sems["v_recv"].at[j]
        first = self.k == 0
        on_x = jnp.logical_and(first, self.x == 0)
        on_z = jnp.logical_and(on_x, self.z == 0)
        plan, base = [], 0
        for on, n, place in (
            (self.root, self.ny, lambda d: self.at(y=d)),
            (on_z, self.nz, lambda d: self.at(z=d)),
            (on_x, self.nx, lambda d: self.at(x=d)),
            (first, 2, lambda d: self.at(k=d)),
        ):
            plan.append((on, [functools.partial(self.remote, chunk, chunk, send.at[j, base + d - 1], recv, place(d)) for d in range(1, n)]))
            base += n - 1
        return plan

    def v_wait(self, j):
        plan = self.v_stages(j)
        pl.when(jnp.logical_not(self.root))(lambda: plan[3][1][0]().wait_recv())

    def v_send(self, j, wait):
        if wait:
            self.v_wait(j)
        for on, copies in self.v_stages(j):
            @pl.when(on)
            def _(copies=copies):
                for copy in copies:
                    copy().start()

    def v_done(self, j):
        for on, copies in self.v_stages(j):
            @pl.when(on)
            def _(copies=copies):
                for copy in copies:
                    copy().wait_send()

    def sequences(self):
        steps = {"x": self.nx // 2, "y": self.ny // 2, "z": self.nz // 2}
        names = (("x0", "y0"), ("y1", "x1"), ("z",))
        return [[(n, t) for n in chain for t in range(1, steps[n[0]] + 1)] for chain in names]

    def slot(self, s):
        r = self.rings()
        for i, chain in enumerate(self.sequences()):
            if s == 0:
                (self.scatter_r_wait if i == 2 else functools.partial(self.scatter_c_wait, i))()
            elif s <= len(chain):
                self.ring_wait(*r[chain[s - 1][0]], chain[s - 1][1])
            if s < len(chain):
                self.ring_start(*r[chain[s][0]], chain[s][1])
            if i == 2 and s == len(chain):
                self.swap_start()
        if s == self.slots() - 1:
            self.swap_wait()

    def slots(self):
        return 1 + max(len(chain) for chain in self.sequences())

    def finish(self):
        r = self.rings()
        for chain in self.sequences():
            for name, step in chain:
                self.ring_done(*r[name], step)
        self.scatter_c_done()
        self.scatter_r_done()
        self.swap_done()
        self.d_done()
        for j in range(8):
            self.v_done(j)


NAMES = ("local", "cs_send", "cs_recv", "rs_send", "rs_recv", "x0", "y0", "y1", "x1", "z", "swap", "d", "v_send", "v_recv")


def semaphores(nx, ny, nz):
    dma = pltpu.SemaphoreType.DMA
    shapes = {
        "local": (6,), "cs_send": (nx * ny,), "cs_recv": (2,), "rs_send": (nz,), "rs_recv": (),
        "x0": (2, 2, nx // 2), "y0": (2, 2, ny // 2), "y1": (2, 2, ny // 2), "x1": (2, 2, nx // 2),
        "z": (2, 2, nz // 2), "swap": (2,), "d": (3,), "v_send": (8, nx + ny + nz - 2), "v_recv": (8,),
    }
    return [dma(shapes[name]) for name in NAMES]


def dot(a, b):
    return jnp.dot(a, b, precision=HI, preferred_element_type=F)


def dot_t(a, b):
    return lax.dot_general(a, b, (((1,), (1,)), ((), ())), precision=HI, preferred_element_type=F)


def t_dot(a, b):
    return lax.dot_general(a, b, (((0,), (0,)), ((), ())), precision=HI, preferred_element_type=F)


def eye(n):
    return (lax.broadcasted_iota(jnp.int32, (n, n), 0) == lax.broadcasted_iota(jnp.int32, (n, n), 1)).astype(F)


def tiles(ref):
    q, _, rows, _ = ref.shape
    return jnp.concatenate([ref[:, ct].reshape(q * rows, 128) for ct in range(2)], axis=1)


def factor(c, s, hook):
    vbuf = c.vbuf
    s[:, 0:W] = eye(W)
    s[:, W:2 * W] = jnp.zeros((W, W), F)
    s[:, 2 * W:3 * W] = tiles(c.rsrc.at[pl.ds(0, 4)])
    for p in range(2):
        if p == 1:
            v00 = s[:, 0:W]
            for b in range(2):
                c.d_copy(b).wait_recv()
            u01 = dot(v00, tiles(c.dbuf.at[0]))
            s[:, 0:W] = -t_dot(u01, v00)
            s[:, W:2 * W] = eye(W)
            s[:, 2 * W:3 * W] = tiles(c.dbuf.at[1]) - t_dot(u01, u01)
        for i in range(4):
            lo, hi = 64 * i, 64 * i + 64
            m = jnp.concatenate([eye(64), s[lo:hi, 2 * W + lo:2 * W + hi]], axis=1)
            rows = leaf([m[8 * v:8 * v + 8, :] for v in range(8)])
            w = jnp.concatenate(rows, axis=0)[:, 0:64]
            r = dot(w, s[lo:hi, :])
            j = 4 * p + i
            vbuf[j, 0] = r[:, 0:W]
            if p == 1:
                vbuf[j, 1] = r[:, W:2 * W]
            c.v_send(j, False)
            if i < 3:
                col = dot_t(s[hi:W, 2 * W + lo:2 * W + hi], w)
                s[hi:W, :] = s[hi:W, :] - dot(col, r)
            s[lo:hi, :] = r
            hook(j)


def split(a):
    high = a.astype(jnp.bfloat16)
    return high, (a - high.astype(F)).astype(jnp.bfloat16)


def v_rows(c, p):
    return [jnp.concatenate([c.vbuf[4 * p + i, k] for i in range(4)], axis=0) for k in range(p + 1)]


def panel_rows(c, p, pr, rcat):
    parts = [dot_t(tiles(c.rbuf.at[k]), v) for k, v in enumerate(v_rows(c, p))]
    own = parts[0] if p == 0 else parts[0] + parts[1]
    pr[p] = own

    @pl.when(c.row < 2)
    def _():
        place = lax.broadcasted_iota(jnp.int32, (W, W), 0) + c.row * W
        keep = place >= lax.broadcasted_iota(jnp.int32, (W, W), 1) + p * W
        pr[p, 0:W] = jnp.where(keep, pr[p, 0:W], 0.0)

    high, low = split(pr[p])
    rcat[:, p * W:(p + 1) * W] = high
    rcat[:, (2 + p) * W:(3 + p) * W] = high
    rcat[:, (4 + p) * W:(5 + p) * W] = low


def panel_columns(c, p, ccat):
    vs = v_rows(c, p)
    for ct in range(2):
        for pair in range(2):
            lanes = [ct * 4 + 2 * pair, ct * 4 + 2 * pair + 1]
            total = None
            for k, v in enumerate(vs):
                a = jnp.concatenate(
                    [c.cbuf[k, :, :, pl.ds(t, 8, stride=8), :].reshape(W, 128) for t in lanes], axis=1
                )
                part = dot(v, a)
                total = part if total is None else total + part
            if pair == 0:
                place = lax.broadcasted_iota(jnp.int32, (W, 2 * 128), 1)
                place = jnp.where(place < 128, place + ct * 128 + c.col * W, 2 * W)
                keep = place >= lax.broadcasted_iota(jnp.int32, (W, 2 * 128), 0) + p * W
                total = jnp.where(keep, total, 0.0)
            high, low = split(total)
            at = slice(lanes[0] * 128, lanes[0] * 128 + 256)
            ccat[p * W:(p + 1) * W, at] = high
            ccat[(2 + p) * W:(3 + p) * W, at] = low
            ccat[(4 + p) * W:(5 + p) * W, at] = high


def update(c, out, pr, rcat, ccat):
    step = 128
    for part in range(4):
        rows = slice(part * step, part * step + step)
        for pair in range(4):
            product = jnp.dot(rcat[rows, :], ccat[:, pair * 256:pair * 256 + 256], preferred_element_type=F)
            for half in range(2):
                at = (pl.ds(part * step * 8 + pair * 2 + half, step, stride=8), slice(None))
                c.hv[at] = c.hv[at] - product[:, half * 128:half * 128 + 128]
        whole = pl.ds(part * step * 8, step * 8)
        if part < 2:
            @pl.when(c.row < 2)
            def _():
                c.hv[whole, :] = jnp.zeros((step * 8, 128), F)
        for p in range(2):
            @pl.when(c.col == p)
            def _(p=p):
                for ct in range(2):
                    c.hv[pl.ds(part * step * 8 + ct * 4, step, stride=8), :] = pr[p, rows, ct * 128:ct * 128 + 128]
        pltpu.make_async_copy(c.hv.at[whole], out.at[whole], c.sems["local"].at[part]).start()
    for part in range(4):
        whole = pl.ds(part * step * 8, step * 8)
        pltpu.make_async_copy(c.hv.at[whole], out.at[whole], c.sems["local"].at[part]).wait()


def kernel(dims, h, out, hv, rsrc, cbuf, rbuf, vbuf, dbuf, s, pr, rcat, ccat, *sems):
    c = Comm(*dims, h, hv, rsrc, cbuf, rbuf, vbuf, dbuf, dict(zip(NAMES, sems)))
    load = pltpu.make_async_copy(h, hv, c.sems["local"].at[3])
    load.start()
    c.barrier()
    load.wait()
    c.prepare()
    c.d_send()
    c.scatter_c()
    c.scatter_r()
    slots = c.slots()

    @pl.when(c.root)
    def _():
        factor(c, s, lambda j: c.slot(j) if j < slots else None)

    @pl.when(jnp.logical_not(c.root))
    def _():
        for j in range(8):
            if j < slots:
                c.slot(j)
            c.v_send(j, True)

    for p in range(2):
        panel_rows(c, p, pr, rcat)
        panel_columns(c, p, ccat)
    update(c, out, pr, rcat, ccat)
    c.finish()


def on_device(dims, hessian):
    i, r, l, w = hessian.shape
    nx, ny, nz = dims
    n = nx * ny
    flat = hessian.reshape(i, r, l, 2, 128).transpose(0, 1, 3, 2, 4).reshape(i * r * 2 * l, 128)
    out = pl.pallas_call(
        functools.partial(kernel, dims),
        out_shape=jax.ShapeDtypeStruct(flat.shape, F),
        in_specs=[pl.BlockSpec(memory_space=pl.ANY)],
        out_specs=pl.BlockSpec(memory_space=pl.ANY),
        scratch_shapes=[
            pltpu.VMEM(flat.shape, F),
            pltpu.VMEM((nz, 2, 2 * W // nz, 128), F),
            pltpu.VMEM((2, nx, ny, W * 8 // n, 128), F),
            pltpu.VMEM((2, nz, 2, 2 * W // nz, 128), F),
            pltpu.VMEM((8, 2, 64, W), F),
            pltpu.VMEM((2, 4, 2, 64, 128), F),
            pltpu.VMEM((W, 3 * W), F),
            pltpu.VMEM((2, 2 * W, W), F),
            pltpu.VMEM((2 * W, 6 * W), jnp.bfloat16),
            pltpu.VMEM((6 * W, 4 * W), jnp.bfloat16),
        ] + semaphores(nx, ny, nz),
        compiler_params=pltpu.CompilerParams(collective_id=0, has_side_effects=True, vmem_limit_bytes=40 << 20),
        name="panels",
    )(flat)
    return out.reshape(i, r, 2, l, 128).transpose(0, 1, 3, 2, 4).reshape(i, r, l, w)


def solution(mesh):
    spec = P(None, "row", None, "col")
    return jax.shard_map(
        functools.partial(on_device, (4, 8, 8)), mesh=mesh, in_specs=(spec,), out_specs=spec, check_vma=False
    )
```

```python
import functools

import jax
import jax.numpy as jnp
from jax import lax
from jax.experimental import pallas as pl
from jax.experimental.pallas import tpu as pltpu
from jax.sharding import PartitionSpec as P

F = jnp.float32
HI = lax.Precision.HIGHEST
MESH = pl.DeviceIdType.MESH
W = 256
SUB = 2
LAG = 1
ROOT_LAG = 3
LEAVES = (3, 5, 6, 7)
RELAY = {1: (0, 2, 3, 4), 2: (1, 3, 4, 5), 3: (2, 4, 5, 6), 4: (3, 5, 6, 7)}


def recip(p):
    r = pl.reciprocal(p, approx=True)
    return r * (2.0 - p * r)

def leaf(m):
    m = list(m)
    sub = lax.broadcasted_iota(jnp.int32, (8, 128), 0)
    out = []
    for g in range(8):
        c = [[jnp.broadcast_to(m[v][:, 64 + 8 * g + k:65 + 8 * g + k], (8, 128)) for v in range(g, 8)] for k in range(8)]
        top = m[g]
        pivots = jnp.ones((8, 128), F)
        scaled_rows = []
        for k in range(8):
            col = c[k]
            pivot = jnp.broadcast_to(col[0][k:k + 1, :], (8, 128))
            r = recip(pivot)
            row = jnp.broadcast_to(top[k:k + 1, :], (8, 128)) * r
            scaled_rows.append(row)
            pivots = jnp.where(sub == k, pivot, pivots)
            top = top - jnp.where(sub > k, col[0], 0.0) * row
            for n in range(k + 1, 8):
                s = jnp.broadcast_to(col[0][n:n + 1, :], (8, 128)) * r
                c[n] = [a - b * s for a, b in zip(c[n], col)]
        for v in range(g + 1, 8):
            acc = m[v]
            for k in range(8):
                acc = acc - c[k][v - g] * scaled_rows[k]
            m[v] = acc
        out.append(top * lax.rsqrt(pivots))
    return out

class Comm:
    def __init__(self, nx, ny, nz, h, hv, rsrc, cbuf, rbuf, vbuf, dbuf, via, sems):
        self.nx, self.ny, self.nz = nx, ny, nz
        self.h, self.hv, self.rsrc, self.cbuf, self.rbuf = h, hv, rsrc, cbuf, rbuf
        self.vbuf, self.dbuf, self.via = vbuf, dbuf, via
        self.sems = sems
        self.row = lax.axis_index("row")
        self.col = lax.axis_index("col")
        self.x, self.y = self.row // ny, self.row % ny
        self.z, self.k = self.col // 2, self.col % 2
        self.root = jnp.logical_and(self.row == 0, self.col == 0)

    def at(self, x=None, y=None, z=None, k=None):
        x = self.x if x is None else x
        y = self.y if y is None else y
        z = self.z if z is None else z
        k = self.k if k is None else k
        return (x * self.ny + y, z * 2 + k)

    def signal(self):
        nx, ny, nz = self.nx, self.ny, self.nz
        sem = pltpu.get_barrier_semaphore()

        def tell(device):
            pl.semaphore_signal(sem, inc=1, device_id=device, device_id_type=MESH)

        for root in range(2):
            pl.when(self.row != root)(lambda root=root: tell((root, self.col)))
        for y in range(2):
            pl.when(jnp.logical_and(self.x != 0, self.y != y))(lambda y=y: tell(self.at(y=y)))
        tell(self.at(k=1 - self.k))
        for d in (1, -1):
            tell(self.at(y=(self.y + d) % ny))
        for d in range(1, nz):
            tell(self.at(z=(self.z + d) % nz))
        for d in range(1, nx):
            tell(self.at(x=(self.x + d) % nx))
        pl.when(self.root)(lambda: tell((1, 1)))

    def barrier(self):
        nx, ny, nz = self.nx, self.ny, self.nz
        total = 5 + nx - 1
        total = total + jnp.where(self.row < 2, nx * ny - 1, 0) + jnp.where(self.z == 0, nz - 1, 0)
        total = total + jnp.where(self.d_source(1), 1, 0)
        total = total + jnp.where(jnp.logical_and(self.x != 0, self.y < 2), ny - 1, 0)
        total = total + nz - 3 - jnp.where(self.z == 0, nz - 1, 0)
        pl.semaphore_wait(pltpu.get_barrier_semaphore(), total)

    def remote(self, src, dst, send, recv, device):
        return pltpu.make_async_remote_copy(
            src_ref=src, dst_ref=dst, send_sem=send, recv_sem=recv, device_id=device, device_id_type=MESH
        )

    def piece_copy(self, root, u, p):
        size = self.cbuf.shape[3] // SUB
        return self.remote(
            self.h.at[pl.ds((p * SUB + u) * size, size)],
            self.cbuf.at[root, p // self.ny, p % self.ny, pl.ds(u * size, size)],
            self.sems["cs_send"].at[u, p], self.sems["cs_recv"].at[u, root], (p, self.col),
        )

    def own_piece(self, root):
        size = self.cbuf.shape[3]
        return pltpu.make_async_copy(
            self.h.at[pl.ds(root * size, size)], self.cbuf.at[root, 0, root], self.sems["local"].at[root]
        )

    def via_copy(self, root, p):
        size = self.cbuf.shape[3] // SUB
        return self.remote(
            self.h.at[pl.ds((p * SUB + 1) * size, size)], self.via.at[p % self.ny],
            self.sems["cs_send"].at[1, p], self.sems["cv_recv"].at[p % self.ny], ((p // self.ny) * self.ny + root, self.col),
        )

    def on_copy(self, root, y):
        size = self.cbuf.shape[3] // SUB
        return self.remote(
            self.via.at[y], self.cbuf.at[root, self.x, y, pl.ds(size, size)],
            self.sems["cs_send"].at[1, y], self.sems["cs_recv"].at[1, root], self.at(y=y))

    def on_own(self, root):
        size = self.cbuf.shape[3] // SUB
        return pltpu.make_async_copy(
            self.via.at[root], self.cbuf.at[root, self.x, root, pl.ds(size, size)], self.sems["local"].at[4])

    def scatter_c(self):
        nx, ny = self.nx, self.ny
        for root in range(2):

            @pl.when(self.row == root)
            def _(root=root):
                self.own_piece(root).start()

                def send(i, carry):
                    p = (i % nx) * ny + (i // nx + root) % ny
                    pl.when(p != root)(self.piece_copy(root, 0, p).start)
                    pl.when(p >= ny)(self.via_copy(root, p).start)
                    pl.when(jnp.logical_and(p < ny, p != root))(self.piece_copy(root, 1, p).start)
                    return carry
                lax.fori_loop(0, nx * ny, send, 0)

    def relays(self, root):
        return jnp.logical_and(self.x != 0, self.y == root)

    def hand_on(self):
        for root in range(2):

            @pl.when(self.relays(root))
            def _(root=root):
                def step(i, carry):
                    y = (i + root) % self.ny
                    self.via_copy(root, self.x * self.ny + y).wait_recv()
                    pl.when(y != root)(self.on_copy(root, y).start)
                    pl.when(y == root)(self.on_own(root).start)
                    return carry
                lax.fori_loop(0, self.ny, step, 0)

    def scatter_c_wait(self, root, u):
        size = self.cbuf.shape[3] // SUB
        if u == 0:
            pl.when(self.row == root)(lambda: self.own_piece(root).wait())
        waits = self.row != root
        if u == 1:
            waits = jnp.logical_and(waits, jnp.logical_not(self.relays(root)))
            pl.when(self.relays(root))(lambda: self.on_own(root).wait())

        @pl.when(waits)
        def _():
            piece = self.cbuf.at[root, self.x, self.y, pl.ds(u * size, size)]
            self.remote(piece, piece, self.sems["cs_send"].at[u, 0], self.sems["cs_recv"].at[u, root], self.at()).wait_recv()

    def scatter_c_done(self):
        for root in range(2):

            @pl.when(self.row == root)
            def _(root=root):
                for u in range(SUB):
                    def done(p, carry, u=u):
                        pl.when(p != root)(self.piece_copy(root, u, p).wait_send)
                        return carry
                    lax.fori_loop(0, self.nx * self.ny, done, 0)

            @pl.when(self.relays(root))
            def _(root=root):
                def done_on(y, carry):
                    pl.when(y != root)(self.on_copy(root, y).wait_send)
                    return carry
                lax.fori_loop(0, self.ny, done_on, 0)

    def scatter_r_copy(self, q):
        return self.remote(
            self.rsrc.at[q], self.rbuf.at[self.k, q], self.sems["rs_send"].at[q], self.sems["rs_recv"], self.at(z=q)
        )

    def scatter_r_local(self):
        return [
            pltpu.make_async_copy(self.rsrc.at[0], self.rbuf.at[kk, 0], self.sems["local"].at[2]) for kk in range(2)
        ]

    def scatter_r(self):
        @pl.when(self.z == 0)
        def _():
            for q in range(1, self.nz):
                self.scatter_r_copy(q).start()
            for kk in range(2):
                pl.when(self.k == kk)(self.scatter_r_local()[kk].start)

    def scatter_r_wait(self):
        @pl.when(self.z == 0)
        def _():
            for kk in range(2):
                pl.when(self.k == kk)(self.scatter_r_local()[kk].wait)

        @pl.when(self.z != 0)
        def _():
            piece = self.rbuf.at[self.k, self.z]
            self.remote(piece, piece, self.sems["rs_send"].at[0], self.sems["rs_recv"], self.at()).wait_recv()

    def scatter_r_done(self):
        @pl.when(self.z == 0)
        def _():
            for q in range(1, self.nz):
                self.scatter_r_copy(q).wait_send()

    def ring(self, name, n, me, device, piece, step):
        half = n // 2
        out = []
        for way, sign in enumerate((1, -1)):
            index = (me - sign * (step - 1)) % n
            ref = piece(index, way if step == half else None)
            send = self.sems[name[0]].at[name[1], 0, way, step - 1]
            recv = self.sems[name[0]].at[name[1], 1, way, step - 1]
            out.append(self.remote(ref, ref, send, recv, device((me + sign) % n)))
        return out

    def ring_start(self, name, *args):
        for copy in self.ring(name, *args):
            copy.start()

    def ring_wait(self, name, n, me, device, piece, step):
        half = n // 2
        for way, sign in enumerate((1, -1)):
            index = (me - sign * step) % n
            ref = piece(index, way if step == half else None)
            send = self.sems[name[0]].at[name[1], 0, way, step - 1]
            recv = self.sems[name[0]].at[name[1], 1, way, step - 1]
            self.remote(ref, ref, send, recv, device((me + sign) % n)).wait_recv()

    def ring_done(self, name, *args):
        for copy in self.ring(name, *args):
            copy.wait_send()

    def rings(self):
        c = self.cbuf
        size = c.shape[3] // SUB
        hy = self.ny // 2

        def part(u, h):
            return pl.ds(u * size, size) if h is None else pl.ds(u * size + h * (size // 2), size // 2)

        out = {}
        for u in range(SUB):
            out["x0", u] = (self.nx, self.x, lambda i: self.at(x=i), lambda i, h, u=u: c.at[0, i, self.y, part(u, h)])
            out["y0", u] = (self.ny, self.y, lambda i: self.at(y=i), lambda i, h, u=u: c.at[0, :, i, part(u, h)])
            out["y1", u] = (self.ny, self.y, lambda i: self.at(y=i), lambda i, h, u=u: c.at[1, self.x, i, part(u, h)])
            out["x1", u] = (self.nx, self.x, lambda i: self.at(x=i), lambda i, h, u=u: c.at[
                1, i, slice(None) if h is None else pl.ds(h * hy, hy), part(u, None)])
        out["z", 0] = (self.nz, self.z, lambda i: self.at(z=i), lambda i, h: (
            self.rbuf.at[self.k, i] if h is None else self.rbuf.at[self.k, i, h]))
        return {key: (key,) + value for key, value in out.items()}

    def swap_copy(self, kk):
        return self.remote(
            self.rbuf.at[kk], self.rbuf.at[kk], self.sems["swap"].at[0], self.sems["swap"].at[1], self.at(k=1 - self.k)
        )

    def swap_start(self):
        for kk in range(2):
            pl.when(self.k == kk)(self.swap_copy(kk).start)

    def swap_wait(self):
        for kk in range(2):
            pl.when(self.k != kk)(self.swap_copy(kk).wait_recv)

    def swap_done(self):
        for kk in range(2):
            pl.when(self.k == kk)(self.swap_copy(kk).wait_send)

    def prepare(self):
        @pl.when(self.z == 0)
        def _():
            nq, _, size, _ = self.rsrc.shape
            for q in range(nq):
                for ct in range(2):
                    self.rsrc[q, ct] = self.hv[pl.ds(q * size * 8 + ct * 4, size, stride=8), :]

    def d_source(self, b):
        return jnp.logical_and(self.row == b, self.col == 1)

    def d_copy(self, b):
        return self.remote(
            self.rsrc.at[pl.ds(0, self.dbuf.shape[1])], self.dbuf.at[b], self.sems["d"].at[0], self.sems["d"].at[1 + b], (0, 0)
        )

    def d_send(self):
        for b in range(2):
            pl.when(self.d_source(b))(lambda b=b: self.d_copy(b).start())

    def d_done(self):
        for b in range(2):
            pl.when(self.d_source(b))(lambda b=b: self.d_copy(b).wait_send())

    def v_part(self, b, i):
        if b == 0:
            return self.vbuf.at[i // 2, 0, pl.ds(pl.multiple_of((i % 2) * 32, 32), 32)]
        if b == 1:
            return self.vbuf.at[4 + i // 4, :, pl.ds(pl.multiple_of((i % 4) * 16, 16), 16)]
        return self.vbuf.at[4 + b, :, pl.ds(pl.multiple_of(i * 8, 8), 8)]

    def v_whole(self, b):
        return (self.vbuf.at[pl.ds(0, 4), 0], self.vbuf.at[pl.ds(4, 2)], self.vbuf.at[6], self.vbuf.at[7])[b]

    def v_plan(self, b):
        nx, ny, nz = self.nx, self.ny, self.nz
        send, recv = self.sems["v_send"], self.sems["v_recv"]
        first = self.k == 0
        on_x = jnp.logical_and(first, self.x == 0)
        on_y = jnp.logical_and(on_x, self.y == 0)

        def copy(i, slot, device):
            part = self.v_part(b, i)
            return functools.partial(self.remote, part, part, send.at[b, slot], recv.at[b, i], device)

        plan = [(self.root, copy(d, d - 1, self.at(z=d))) for d in range(1, nz)]
        base = nz - 2
        plan += [(on_y, copy(self.z, base + d, self.at(y=d))) for d in range(1, ny)]
        base += ny - 1
        plan += [(on_x, copy(self.z, base + d, self.at(x=d))) for d in range(1, nx)]
        base += nx - 1
        for d in range(1, nz):
            z = (self.z + d) % nz
            to = jnp.logical_and(first, jnp.logical_or(self.row != 0, z != 0))
            plan.append((to, copy(self.z, base + d, self.at(z=z))))
        return plan

    def v_swap(self, b):
        whole = self.v_whole(b)
        return self.remote(whole, whole, self.sems["v_swap"].at[0, b], self.sems["v_swap"].at[1, b], self.at(k=1 - self.k))

    def v_relay(self, b):
        part = self.v_part(b, self.z)

        @pl.when(jnp.logical_and(self.k == 0, jnp.logical_not(self.root)))
        def _():
            self.remote(part, part, self.sems["v_send"].at[b, 0], self.sems["v_recv"].at[b, self.z], self.at()).wait_recv()

        for on, copy in self.v_plan(b):
            pl.when(on)(lambda copy=copy: copy().start())

    def v_collect(self, b):
        @pl.when(self.k == 0)
        def _():
            @pl.when(jnp.logical_not(self.root))
            def _():
                for d in range(1, self.nz):
                    z = (self.z + d) % self.nz
                    part = self.v_part(b, z)
                    self.remote(part, part, self.sems["v_send"].at[b, 0], self.sems["v_recv"].at[b, z], self.at()).wait_recv()
            self.v_swap(b).start()

    def v_wait(self, b):
        pl.when(self.k == 1)(lambda: self.v_swap(b).wait_recv())

    def v_done(self, b):
        for on, copy in self.v_plan(b):
            pl.when(on)(lambda copy=copy: copy().wait_send())
        pl.when(self.k == 0)(lambda: self.v_swap(b).wait_send())

    def depth(self, d):
        on_x = self.x == 0
        on_y = jnp.logical_and(on_x, self.y == 0)
        return jnp.logical_and(self.k == 0, (
            None, jnp.logical_and(on_y, self.z != 0), jnp.logical_and(on_x, self.y != 0), self.x != 0)[d])

    def sequences(self):
        steps = {"x": self.nx // 2, "y": self.ny // 2, "z": self.nz // 2}
        chains = []
        for u in range(SUB):
            for root, names in enumerate((("x0", "y0"), ("y1", "x1"))):
                first = functools.partial(self.scatter_c_wait, root, u)
                chains.append((u * LAG, first, [((n, u), t) for n in names for t in range(1, steps[n[0]] + 1)]))
        chains.append((0, self.scatter_r_wait, [(("z", 0), t) for t in range(1, steps["z"] + 1)]))
        return chains

    def slot(self, slot):
        r = self.rings()
        for begin, first, chain in self.sequences():
            s = slot - begin
            if s == 0:
                first()
            elif 0 < s <= len(chain):
                self.ring_wait(*r[chain[s - 1][0]], chain[s - 1][1])
            if 0 <= s < len(chain):
                self.ring_start(*r[chain[s][0]], chain[s][1])
            if s == len(chain) and chain[0][0][0] == "z":
                self.swap_start()
        if slot == self.slots() - 1:
            self.swap_wait()

    def slots(self):
        return 1 + max(begin + len(chain) for begin, _, chain in self.sequences())

    def finish(self):
        r = self.rings()
        for _, _, chain in self.sequences():
            for name, step in chain:
                self.ring_done(*r[name], step)
        self.scatter_c_done()
        self.scatter_r_done()
        self.swap_done()
        self.d_done()
        for b in range(4):
            self.v_done(b)


NAMES = ("local", "cs_send", "cs_recv", "rs_send", "rs_recv", "x0", "y0", "y1", "x1", "z", "swap", "d", "v_send", "v_recv", "v_swap", "cv_recv")


def semaphores(nx, ny, nz):
    dma = pltpu.SemaphoreType.DMA
    shapes = {
        "local": (6,), "cs_send": (SUB, nx * ny), "cs_recv": (SUB, 2), "rs_send": (nz,), "rs_recv": (),
        "x0": (SUB, 2, 2, nx // 2), "y0": (SUB, 2, 2, ny // 2), "y1": (SUB, 2, 2, ny // 2), "x1": (SUB, 2, 2, nx // 2),
        "z": (1, 2, 2, nz // 2), "swap": (2,), "d": (3,), "v_send": (4, nx + ny + 2 * nz - 4), "v_recv": (4, nz), "v_swap": (2, 4),
        "cv_recv": (ny,),
    }
    return [dma(shapes[name]) for name in NAMES]


def dot(a, b):
    return jnp.dot(a, b, precision=HI, preferred_element_type=F)


def dot_t(a, b):
    return lax.dot_general(a, b, (((1,), (1,)), ((), ())), precision=HI, preferred_element_type=F)


def t_dot(a, b):
    return lax.dot_general(a, b, (((0,), (0,)), ((), ())), precision=HI, preferred_element_type=F)


def eye(n):
    return (lax.broadcasted_iota(jnp.int32, (n, n), 0) == lax.broadcasted_iota(jnp.int32, (n, n), 1)).astype(F)


def tiles(ref):
    q, _, rows, _ = ref.shape
    return jnp.concatenate([ref[:, ct].reshape(q * rows, 128) for ct in range(2)], axis=1)


def factor(c, s, begin, hook):
    vbuf = c.vbuf
    s[:, 0:W] = eye(W)
    s[:, W:2 * W] = jnp.zeros((W, W), F)
    s[:, 2 * W:3 * W] = tiles(c.rsrc.at[pl.ds(0, 4)])
    for p in range(2):
        if p == 1:
            v00 = s[:, 0:W]
            for b in range(2):
                c.d_copy(b).wait_recv()
            u01 = dot(v00, tiles(c.dbuf.at[0]))
            s[:, 0:W] = -t_dot(u01, v00)
            s[:, W:2 * W] = eye(W)
            s[:, 2 * W:3 * W] = tiles(c.dbuf.at[1]) - t_dot(u01, u01)
        for i in range(4):
            lo, hi = 64 * i, 64 * i + 64
            m = jnp.concatenate([eye(64), s[lo:hi, 2 * W + lo:2 * W + hi]], axis=1)
            rows = leaf([m[8 * v:8 * v + 8, :] for v in range(8)])
            w = jnp.concatenate(rows, axis=0)[:, 0:64]
            r = dot(w, s[lo:hi, :])
            j = 4 * p + i
            vbuf[j, 0] = r[:, 0:W]
            if p == 1:
                vbuf[j, 1] = r[:, W:2 * W]
            if j == 0:
                begin()
            if j in LEAVES:
                c.v_relay(LEAVES.index(j))
                c.v_collect(LEAVES.index(j))
            if i < 3:
                col = dot_t(s[hi:W, 2 * W + lo:2 * W + hi], w)
                s[hi:W, :] = s[hi:W, :] - dot(col, r)
            s[lo:hi, :] = r
            hook(j)


def split(a):
    high = a.astype(jnp.bfloat16)
    return high, (a - high.astype(F)).astype(jnp.bfloat16)


def v_rows(c, p):
    return [jnp.concatenate([c.vbuf[4 * p + i, k] for i in range(4)], axis=0) for k in range(p + 1)]


def panel_rows(c, p, pr, rcat):
    parts = [dot_t(tiles(c.rbuf.at[k]), v) for k, v in enumerate(v_rows(c, p))]
    own = parts[0] if p == 0 else parts[0] + parts[1]
    pr[p] = own

    @pl.when(c.row < 2)
    def _():
        place = lax.broadcasted_iota(jnp.int32, (W, W), 0) + c.row * W
        keep = place >= lax.broadcasted_iota(jnp.int32, (W, W), 1) + p * W
        pr[p, 0:W] = jnp.where(keep, pr[p, 0:W], 0.0)

    high, low = split(pr[p])
    rcat[:, p * W:(p + 1) * W] = high
    rcat[:, (2 + p) * W:(3 + p) * W] = high
    rcat[:, (4 + p) * W:(5 + p) * W] = low


def panel_columns(c, p, ccat):
    vs = v_rows(c, p)
    for ct in range(2):
        for pair in range(2):
            lanes = [ct * 4 + 2 * pair, ct * 4 + 2 * pair + 1]
            total = None
            for k, v in enumerate(vs):
                a = jnp.concatenate(
                    [c.cbuf[k, :, :, pl.ds(t, 8, stride=8), :].reshape(W, 128) for t in lanes], axis=1
                )
                part = dot(v, a)
                total = part if total is None else total + part
            if pair == 0:
                place = lax.broadcasted_iota(jnp.int32, (W, 2 * 128), 1)
                place = jnp.where(place < 128, place + ct * 128 + c.col * W, 2 * W)
                keep = place >= lax.broadcasted_iota(jnp.int32, (W, 2 * 128), 0) + p * W
                total = jnp.where(keep, total, 0.0)
            high, low = split(total)
            at = slice(lanes[0] * 128, lanes[0] * 128 + 256)
            ccat[p * W:(p + 1) * W, at] = high
            ccat[(2 + p) * W:(3 + p) * W, at] = low
            ccat[(4 + p) * W:(5 + p) * W, at] = high


def update(c, out, pr, rcat, ccat):
    step = 128
    for part in range(4):
        rows = slice(part * step, part * step + step)
        for pair in range(4):
            product = jnp.dot(rcat[rows, :], ccat[:, pair * 256:pair * 256 + 256], preferred_element_type=F)
            for half in range(2):
                at = (pl.ds(part * step * 8 + pair * 2 + half, step, stride=8), slice(None))
                c.hv[at] = c.hv[at] - product[:, half * 128:half * 128 + 128]
        whole = pl.ds(part * step * 8, step * 8)
        if part < 2:
            @pl.when(c.row < 2)
            def _():
                c.hv[whole, :] = jnp.zeros((step * 8, 128), F)
        for p in range(2):
            @pl.when(c.col == p)
            def _(p=p):
                for ct in range(2):
                    c.hv[pl.ds(part * step * 8 + ct * 4, step, stride=8), :] = pr[p, rows, ct * 128:ct * 128 + 128]
        pltpu.make_async_copy(c.hv.at[whole], out.at[whole], c.sems["local"].at[part]).start()
    for part in range(4):
        whole = pl.ds(part * step * 8, step * 8)
        pltpu.make_async_copy(c.hv.at[whole], out.at[whole], c.sems["local"].at[part]).wait()


def kernel(dims, h, out, hv, rsrc, cbuf, rbuf, vbuf, dbuf, via, s, pr, rcat, ccat, *sems):
    c = Comm(*dims, h, hv, rsrc, cbuf, rbuf, vbuf, dbuf, via, dict(zip(NAMES, sems)))
    load = pltpu.make_async_copy(h, hv, c.sems["local"].at[3])
    load.start()
    c.signal()
    load.wait()
    c.prepare()

    def begin():
        c.barrier()
        c.d_send()
        c.scatter_c()
        c.scatter_r()
        c.hand_on()

    slots = c.slots()

    @pl.when(c.root)
    def _():
        def hook(j):
            if j >= ROOT_LAG:
                c.slot(j - ROOT_LAG)
        factor(c, s, begin, hook)
        for t in range(8 - ROOT_LAG, slots):
            c.slot(t)

    @pl.when(jnp.logical_not(c.root))
    def _():
        begin()
        for t in range(slots):
            c.slot(t)
            for depth in (1, 2, 3):
                for b in range(4):
                    if RELAY[depth][b] == t:
                        pl.when(c.depth(depth))(lambda b=b: c.v_relay(b))
            for b in range(4):
                if RELAY[4][b] == t:
                    c.v_collect(b)
        for b in range(4):
            c.v_wait(b)

    for p in range(2):
        panel_rows(c, p, pr, rcat)
        panel_columns(c, p, ccat)
    update(c, out, pr, rcat, ccat)
    c.finish()


def on_device(dims, hessian):
    i, r, l, w = hessian.shape
    nx, ny, nz = dims
    n = nx * ny
    flat = hessian.reshape(i, r, l, 2, 128).transpose(0, 1, 3, 2, 4).reshape(i * r * 2 * l, 128)
    out = pl.pallas_call(
        functools.partial(kernel, dims),
        out_shape=jax.ShapeDtypeStruct(flat.shape, F),
        in_specs=[pl.BlockSpec(memory_space=pltpu.HBM)],
        out_specs=pl.BlockSpec(memory_space=pl.ANY),
        scratch_shapes=[
            pltpu.VMEM(flat.shape, F),
            pltpu.VMEM((nz, 2, 2 * W // nz, 128), F),
            pltpu.VMEM((2, nx, ny, W * 8 // n, 128), F),
            pltpu.VMEM((2, nz, 2, 2 * W // nz, 128), F),
            pltpu.VMEM((8, 2, 64, W), F),
            pltpu.VMEM((2, 4, 2, 64, 128), F),
            pltpu.VMEM((ny, W * 8 // n // SUB, 128), F),
            pltpu.VMEM((W, 3 * W), F),
            pltpu.VMEM((2, 2 * W, W), F),
            pltpu.VMEM((2 * W, 6 * W), jnp.bfloat16),
            pltpu.VMEM((6 * W, 4 * W), jnp.bfloat16),
        ] + semaphores(nx, ny, nz),
        compiler_params=pltpu.CompilerParams(collective_id=0, has_side_effects=True, vmem_limit_bytes=40 << 20),
        name="panels",
    )(flat)
    return out.reshape(i, r, 2, l, 128).transpose(0, 1, 3, 2, 4).reshape(i, r, l, w)


def solution(mesh):
    spec = P(None, "row", None, "col")
    return jax.shard_map(
        functools.partial(on_device, (4, 8, 8)), mesh=mesh, in_specs=(spec,), out_specs=spec, check_vma=False
    )
```

```python
import functools

import jax
import jax.numpy as jnp
from jax import lax
from jax.experimental import pallas as pl
from jax.experimental.pallas import tpu as pltpu
from jax.sharding import PartitionSpec as P

F = jnp.float32
HI = lax.Precision.HIGHEST
MESH = pl.DeviceIdType.MESH
W = 256
SUB = 2
ROOT = {4: (0,), 6: (1,), 7: (2,)}
LEAVES = (3, 5, 6, 7)
RELAY = {1: (0, 1, 2, 3), 2: (1, 2, 3, 4), 3: (2, 3, 4, 5), 4: (3, 4, 5, 9)}


def recip(p):
    r = pl.reciprocal(p, approx=True)
    return r * (2.0 - p * r)

def leaf(m):
    m = list(m)
    sub = lax.broadcasted_iota(jnp.int32, (8, 128), 0)
    out = []
    for g in range(8):
        c = [[jnp.broadcast_to(m[v][:, 64 + 8 * g + k:65 + 8 * g + k], (8, 128)) for v in range(g, 8)] for k in range(8)]
        top = m[g]
        pivots = jnp.ones((8, 128), F)
        scaled_rows = []
        for k in range(8):
            col = c[k]
            pivot = jnp.broadcast_to(col[0][k:k + 1, :], (8, 128))
            r = recip(pivot)
            row = jnp.broadcast_to(top[k:k + 1, :], (8, 128)) * r
            scaled_rows.append(row)
            pivots = jnp.where(sub == k, pivot, pivots)
            top = top - jnp.where(sub > k, col[0], 0.0) * row
            for n in range(k + 1, 8):
                s = jnp.broadcast_to(col[0][n:n + 1, :], (8, 128)) * r
                c[n] = [a - b * s for a, b in zip(c[n], col)]
        for v in range(g + 1, 8):
            acc = m[v]
            for k in range(8):
                acc = acc - c[k][v - g] * scaled_rows[k]
            m[v] = acc
        out.append(top * lax.rsqrt(pivots))
    return out

class Comm:
    def __init__(self, nx, ny, nz, h, hv, rsrc, cbuf, rbuf, vbuf, dbuf, via, sems):
        self.nx, self.ny, self.nz = nx, ny, nz
        self.h, self.hv, self.rsrc, self.cbuf, self.rbuf = h, hv, rsrc, cbuf, rbuf
        self.vbuf, self.dbuf, self.via = vbuf, dbuf, via
        self.sems = sems
        self.row = lax.axis_index("row")
        self.col = lax.axis_index("col")
        self.x, self.y = self.row // ny, self.row % ny
        self.z, self.k = self.col // 2, self.col % 2
        self.root = jnp.logical_and(self.row == 0, self.col == 0)

    def at(self, x=None, y=None, z=None, k=None):
        x = self.x if x is None else x
        y = self.y if y is None else y
        z = self.z if z is None else z
        k = self.k if k is None else k
        return (x * self.ny + y, z * 2 + k)

    def signal(self):
        nx, ny, nz = self.nx, self.ny, self.nz
        sem = pltpu.get_barrier_semaphore()

        def tell(device):
            pl.semaphore_signal(sem, inc=1, device_id=device, device_id_type=MESH)

        for root in range(2):
            pl.when(self.row != root)(lambda root=root: tell((root, self.col)))
        tell(self.at(k=1 - self.k))
        for d in range(1, ny):
            tell(self.at(y=(self.y + d) % ny))
        for d in range(1, nz):
            tell(self.at(z=(self.z + d) % nz))
        for d in range(1, nx):
            tell(self.at(x=(self.x + d) % nx))
        pl.when(self.root)(lambda: tell((1, 1)))
        pl.when(jnp.logical_and(jnp.logical_and(self.row == 0, self.k == 1), self.z != 0))(lambda: tell((0, 0)))

    def barrier(self):
        nx, ny, nz = self.nx, self.ny, self.nz
        total = nx + ny + nz - 2 + jnp.where(self.row < 2, nx * ny - 1, 0) + jnp.where(self.d_source(1), 1, 0)
        total = total + jnp.where(self.root, nz - 1, 0)
        pl.semaphore_wait(pltpu.get_barrier_semaphore(), total)

    def remote(self, src, dst, send, recv, device):
        return pltpu.make_async_remote_copy(
            src_ref=src, dst_ref=dst, send_sem=send, recv_sem=recv, device_id=device, device_id_type=MESH
        )

    def piece_copy(self, root, u, p):
        size = self.cbuf.shape[3] // SUB
        return self.remote(
            self.h.at[pl.ds((p * SUB + u) * size, size)],
            self.cbuf.at[root, p // self.ny, p % self.ny, pl.ds(u * size, size)],
            self.sems["cs_send"].at[u, p], self.sems["cs_recv"].at[u, root], (p, self.col),
        )

    def own_piece(self, root):
        size = self.cbuf.shape[3]
        return pltpu.make_async_copy(
            self.h.at[pl.ds(root * size, size)], self.cbuf.at[root, 0, root], self.sems["local"].at[root]
        )

    def via_copy(self, root, p):
        size = self.cbuf.shape[3] // SUB
        return self.remote(
            self.h.at[pl.ds((p * SUB + 1) * size, size)], self.via.at[p % self.ny],
            self.sems["cs_send"].at[1, p], self.sems["cv_recv"].at[p % self.ny], ((p // self.ny) * self.ny + root, self.col),
        )

    def on_copy(self, root, y):
        size = self.cbuf.shape[3] // SUB
        return self.remote(
            self.via.at[y], self.cbuf.at[root, self.x, y, pl.ds(size, size)],
            self.sems["cs_send"].at[1, y], self.sems["cs_recv"].at[1, root], self.at(y=y))

    def on_own(self, root):
        size = self.cbuf.shape[3] // SUB
        return pltpu.make_async_copy(
            self.via.at[root], self.cbuf.at[root, self.x, root, pl.ds(size, size)], self.sems["local"].at[4])

    def scatter_c(self):
        nx, ny = self.nx, self.ny
        for root in range(2):

            @pl.when(self.row == root)
            def _(root=root):
                self.own_piece(root).start()

                def send(i, carry):
                    p = (i % nx) * ny + (i // nx + root) % ny
                    pl.when(p != root)(self.piece_copy(root, 0, p).start)
                    pl.when(p >= ny)(self.via_copy(root, p).start)
                    pl.when(jnp.logical_and(p < ny, p != root))(self.piece_copy(root, 1, p).start)
                    return carry
                lax.fori_loop(0, nx * ny, send, 0)

    def relays(self, root):
        return jnp.logical_and(self.x != 0, self.y == root)

    def hand_on(self):
        for root in range(2):

            @pl.when(self.relays(root))
            def _(root=root):
                def step(i, carry):
                    y = (i + root) % self.ny
                    self.via_copy(root, self.x * self.ny + y).wait_recv()
                    pl.when(y != root)(self.on_copy(root, y).start)
                    pl.when(y == root)(self.on_own(root).start)
                    return carry
                lax.fori_loop(0, self.ny, step, 0)

    def scatter_c_wait(self, root, u):
        size = self.cbuf.shape[3] // SUB
        if u == 0:
            pl.when(self.row == root)(lambda: self.own_piece(root).wait())
        waits = self.row != root
        if u == 1:
            waits = jnp.logical_and(waits, jnp.logical_not(self.relays(root)))
            pl.when(self.relays(root))(lambda: self.on_own(root).wait())

        @pl.when(waits)
        def _():
            piece = self.cbuf.at[root, self.x, self.y, pl.ds(u * size, size)]
            self.remote(piece, piece, self.sems["cs_send"].at[u, 0], self.sems["cs_recv"].at[u, root], self.at()).wait_recv()

    def scatter_c_done(self):
        for root in range(2):

            @pl.when(self.row == root)
            def _(root=root):
                for u in range(SUB):
                    def done(p, carry, u=u):
                        pl.when(p != root)(self.piece_copy(root, u, p).wait_send)
                        return carry
                    lax.fori_loop(0, self.nx * self.ny, done, 0)

            @pl.when(self.relays(root))
            def _(root=root):
                def done_on(y, carry):
                    pl.when(y != root)(self.on_copy(root, y).wait_send)
                    return carry
                lax.fori_loop(0, self.ny, done_on, 0)

    def scatter_r_copy(self, q):
        return self.remote(
            self.rsrc.at[q], self.rbuf.at[self.k, q], self.sems["rs_send"].at[q], self.sems["rs_recv"], self.at(z=q)
        )

    def scatter_r_local(self):
        return [
            pltpu.make_async_copy(self.rsrc.at[0], self.rbuf.at[kk, 0], self.sems["local"].at[2]) for kk in range(2)
        ]

    def scatter_r(self):
        @pl.when(self.z == 0)
        def _():
            for q in range(1, self.nz):
                self.scatter_r_copy(q).start()
            for kk in range(2):
                pl.when(self.k == kk)(self.scatter_r_local()[kk].start)

    def scatter_r_wait(self):
        @pl.when(self.z == 0)
        def _():
            for kk in range(2):
                pl.when(self.k == kk)(self.scatter_r_local()[kk].wait)

        @pl.when(self.z != 0)
        def _():
            piece = self.rbuf.at[self.k, self.z]
            self.remote(piece, piece, self.sems["rs_send"].at[0], self.sems["rs_recv"], self.at()).wait_recv()

    def scatter_r_done(self):
        @pl.when(self.z == 0)
        def _():
            for q in range(1, self.nz):
                self.scatter_r_copy(q).wait_send()

    def ring(self, name, n, me, device, piece, step):
        half = n // 2
        out = []
        for way, sign in enumerate((1, -1)):
            index = (me - sign * (step - 1)) % n
            ref = piece(index, way if step == half else None)
            send = self.sems[name].at[0, way, step - 1]
            recv = self.sems[name].at[1, way, step - 1]
            out.append(self.remote(ref, ref, send, recv, device((me + sign) % n)))
        return out

    def ring_start(self, name, *args):
        for copy in self.ring(name, *args):
            copy.start()

    def ring_wait(self, name, n, me, device, piece, step):
        half = n // 2
        for way, sign in enumerate((1, -1)):
            index = (me - sign * step) % n
            ref = piece(index, way if step == half else None)
            send = self.sems[name].at[0, way, step - 1]
            recv = self.sems[name].at[1, way, step - 1]
            self.remote(ref, ref, send, recv, device((me + sign) % n)).wait_recv()

    def ring_done(self, name, *args):
        for copy in self.ring(name, *args):
            copy.wait_send()

    def direct(self, name, n, me, device, piece, d):
        ref = piece(me, None)
        return self.remote(ref, ref, self.sems[name].at[0, d], self.sems[name].at[1, d], device((me + d) % n))

    def direct_start(self, name, n, *args):
        for d in range(1, n):
            self.direct(name, n, *args, d).start()

    def direct_wait(self, name, n, me, device, piece):
        for d in range(1, n):
            ref = piece((me - d) % n, None)
            self.remote(ref, ref, self.sems[name].at[0, d], self.sems[name].at[1, d], device((me + d) % n)).wait_recv()

    def direct_done(self, name, n, *args):
        for d in range(1, n):
            self.direct(name, n, *args, d).wait_send()

    def rings(self):
        c = self.cbuf
        size, hy = c.shape[3] // 2, self.ny // 2

        def part(h):
            return slice(None) if h is None else pl.ds(h * size, size)

        out = {
            "x0": (self.nx, self.x, lambda i: self.at(x=i), lambda i, h: c.at[0, i, self.y]),
            "y0": (self.ny, self.y, lambda i: self.at(y=i), lambda i, h: c.at[0, :, i, part(h)]),
            "y1": (self.ny, self.y, lambda i: self.at(y=i), lambda i, h: c.at[1, self.x, i]),
            "x1": (self.nx, self.x, lambda i: self.at(x=i), lambda i, h: c.at[1, i, slice(None) if h is None else pl.ds(h * hy, hy)]),
            "z": (self.nz, self.z, lambda i: self.at(z=i), lambda i, h: self.rbuf.at[self.k, i]),
        }
        return {key: (key,) + value for key, value in out.items()}

    def swap_copy(self, kk):
        return self.remote(
            self.rbuf.at[kk], self.rbuf.at[kk], self.sems["swap"].at[0], self.sems["swap"].at[1], self.at(k=1 - self.k)
        )

    def swap_start(self):
        for kk in range(2):
            pl.when(self.k == kk)(self.swap_copy(kk).start)

    def swap_wait(self):
        for kk in range(2):
            pl.when(self.k != kk)(self.swap_copy(kk).wait_recv)

    def swap_done(self):
        for kk in range(2):
            pl.when(self.k == kk)(self.swap_copy(kk).wait_send)

    def prepare(self):
        @pl.when(self.z == 0)
        def _():
            nq, _, size, _ = self.rsrc.shape
            for q in range(nq):
                for ct in range(2):
                    self.rsrc[q, ct] = self.hv[pl.ds(q * size * 8 + ct * 4, size, stride=8), :]

    def d_source(self, b):
        return jnp.logical_and(self.row == b, self.col == 1)

    def d_copy(self, b):
        return self.remote(
            self.rsrc.at[pl.ds(0, self.dbuf.shape[1])], self.dbuf.at[b], self.sems["d"].at[0], self.sems["d"].at[1 + b], (0, 0)
        )

    def d_send(self):
        for b in range(2):
            pl.when(self.d_source(b))(lambda b=b: self.d_copy(b).start())

    def d_done(self):
        for b in range(2):
            pl.when(self.d_source(b))(lambda b=b: self.d_copy(b).wait_send())

    def v_part(self, b, i):
        if b == 0:
            return self.vbuf.at[i // 2, 0, pl.ds(pl.multiple_of((i % 2) * 32, 32), 32)]
        if b == 1:
            return self.vbuf.at[4 + i // 4, :, pl.ds(pl.multiple_of((i % 4) * 16, 16), 16)]
        return self.vbuf.at[4 + b, :, pl.ds(pl.multiple_of(i * 8, 8), 8)]

    def v_whole(self, b):
        return (self.vbuf.at[pl.ds(0, 4), 0], self.vbuf.at[pl.ds(4, 2)], self.vbuf.at[6], self.vbuf.at[7])[b]

    def v_plan(self, b):
        nx, ny, nz = self.nx, self.ny, self.nz
        send, recv = self.sems["v_send"], self.sems["v_recv"]
        core = b % 2
        first = self.k == core
        on_x = jnp.logical_and(first, self.x == 0)
        on_y = jnp.logical_and(on_x, self.y == 0)

        def copy(i, slot, device):
            part = self.v_part(b, i)
            return functools.partial(self.remote, part, part, send.at[b, slot], recv.at[b, i], device)

        plan = [(self.root, copy(d, d, self.at(z=d, k=core))) for d in range(1 - core, nz)]
        base = nz - 1
        plan += [(on_y, copy(self.z, base + d, self.at(y=d))) for d in range(1, ny)]
        base += ny - 1
        plan += [(on_x, copy(self.z, base + d, self.at(x=d))) for d in range(1, nx)]
        base += nx - 1
        for d in range(1, nz):
            z = (self.z + d) % nz
            to = first if core else jnp.logical_and(first, jnp.logical_or(self.row != 0, z != 0))
            plan.append((to, copy(self.z, base + d, self.at(z=z))))
        return plan

    def v_swap(self, b):
        whole = self.v_whole(b)
        return self.remote(whole, whole, self.sems["v_swap"].at[0, b], self.sems["v_swap"].at[1, b], self.at(k=1 - self.k))

    def v_swaps(self, b):
        if b % 2 == 0:
            return self.k == 0
        return jnp.logical_and(self.k == 1, jnp.logical_or(self.row != 0, self.z != 0))

    def v_relay(self, b):
        part = self.v_part(b, self.z)

        @pl.when(jnp.logical_and(self.k == b % 2, jnp.logical_not(self.root)))
        def _():
            self.remote(part, part, self.sems["v_send"].at[b, 0], self.sems["v_recv"].at[b, self.z], self.at()).wait_recv()

        for on, copy in self.v_plan(b):
            pl.when(on)(lambda copy=copy: copy().start())

    def v_collect(self, b):
        @pl.when(jnp.logical_and(self.k == b % 2, jnp.logical_not(self.root)))
        def _():
            for d in range(1, self.nz):
                z = (self.z + d) % self.nz
                part = self.v_part(b, z)
                self.remote(part, part, self.sems["v_send"].at[b, 0], self.sems["v_recv"].at[b, z], self.at()).wait_recv()
        pl.when(self.v_swaps(b))(lambda: self.v_swap(b).start())

    def v_wait(self, b):
        pl.when(jnp.logical_and(self.k != b % 2, jnp.logical_not(self.root)))(lambda: self.v_swap(b).wait_recv())

    def v_done(self, b):
        for on, copy in self.v_plan(b):
            pl.when(on)(lambda copy=copy: copy().wait_send())
        pl.when(self.v_swaps(b))(lambda: self.v_swap(b).wait_send())

    def depth(self, d, b):
        on_x = self.x == 0
        on_y = jnp.logical_and(on_x, self.y == 0)
        first = jnp.logical_and(on_y, self.z != 0) if b % 2 == 0 else on_y
        return jnp.logical_and(self.k == b % 2, (None, first, jnp.logical_and(on_x, self.y != 0), self.x != 0)[d])

    def sequences(self):
        steps = {"x1": self.nx // 2, "y0": self.ny // 2}
        return [[(one, 0)] + [(ring, t) for t in range(1, steps[ring] + 1)] for one, ring in (("x0", "y0"), ("y1", "x1"))]

    def slot(self, slot):
        r = self.rings()
        chains = self.sequences()
        if slot == 0:
            for root in range(2):
                for u in range(SUB):
                    self.scatter_c_wait(root, u)
                self.direct_start(*r[chains[root][0][0]])
            self.scatter_r_wait()
            self.direct_start(*r["z"])
        for chain in chains:
            if 0 < slot <= len(chain):
                name, step = chain[slot - 1]
                self.direct_wait(*r[name]) if step == 0 else self.ring_wait(*r[name], step)
            if 0 < slot < len(chain):
                self.ring_start(*r[chain[slot][0]], chain[slot][1])
        if slot == 2:
            self.direct_wait(*r["z"])
            self.swap_start()
        if slot == self.slots() - 1:
            self.swap_wait()

    def slots(self):
        return 1 + max(len(chain) for chain in self.sequences())

    def finish(self):
        r = self.rings()
        for chain in self.sequences():
            for name, step in chain:
                self.direct_done(*r[name]) if step == 0 else self.ring_done(*r[name], step)
        self.direct_done(*r["z"])
        self.scatter_c_done()
        self.scatter_r_done()
        self.swap_done()
        self.d_done()
        for b in range(4):
            self.v_done(b)


NAMES = ("local", "cs_send", "cs_recv", "rs_send", "rs_recv", "x0", "y0", "y1", "x1", "z", "swap", "d", "v_send", "v_recv", "v_swap", "cv_recv")


def semaphores(nx, ny, nz):
    dma = pltpu.SemaphoreType.DMA
    shapes = {
        "local": (6,), "cs_send": (SUB, nx * ny), "cs_recv": (SUB, 2), "rs_send": (nz,), "rs_recv": (),
        "x0": (2, nx), "y0": (2, 2, ny // 2), "y1": (2, ny), "x1": (2, 2, nx // 2),
        "z": (2, nz), "swap": (2,), "d": (3,), "v_send": (4, nx + ny + 2 * nz - 3), "v_recv": (4, nz), "v_swap": (2, 4),
        "cv_recv": (ny,),
    }
    return [dma(shapes[name]) for name in NAMES]


def dot(a, b):
    return jnp.dot(a, b, precision=HI, preferred_element_type=F)


def dot_t(a, b):
    return lax.dot_general(a, b, (((1,), (1,)), ((), ())), precision=HI, preferred_element_type=F)


def t_dot(a, b):
    return lax.dot_general(a, b, (((0,), (0,)), ((), ())), precision=HI, preferred_element_type=F)


def eye(n):
    return (lax.broadcasted_iota(jnp.int32, (n, n), 0) == lax.broadcasted_iota(jnp.int32, (n, n), 1)).astype(F)


def tiles(ref):
    q, _, rows, _ = ref.shape
    return jnp.concatenate([ref[:, ct].reshape(q * rows, 128) for ct in range(2)], axis=1)


def factor(c, s, begin, hook):
    vbuf = c.vbuf
    s[:, 0:W] = eye(W)
    s[:, W:2 * W] = jnp.zeros((W, W), F)
    s[:, 2 * W:3 * W] = tiles(c.rsrc.at[pl.ds(0, 4)])
    for p in range(2):
        if p == 1:
            v00 = s[:, 0:W]
            for b in range(2):
                c.d_copy(b).wait_recv()
            u01 = dot(v00, tiles(c.dbuf.at[0]))
            s[:, 0:W] = -t_dot(u01, v00)
            s[:, W:2 * W] = eye(W)
            s[:, 2 * W:3 * W] = tiles(c.dbuf.at[1]) - t_dot(u01, u01)
        for i in range(4):
            lo, hi = 64 * i, 64 * i + 64
            m = jnp.concatenate([eye(64), s[lo:hi, 2 * W + lo:2 * W + hi]], axis=1)
            rows = leaf([m[8 * v:8 * v + 8, :] for v in range(8)])
            w = jnp.concatenate(rows, axis=0)[:, 0:64]
            r = dot(w, s[lo:hi, :])
            j = 4 * p + i
            vbuf[j, 0] = r[:, 0:W]
            if p == 1:
                vbuf[j, 1] = r[:, W:2 * W]
            if j == 0:
                begin()
            if j in LEAVES:
                c.v_relay(LEAVES.index(j))
                c.v_collect(LEAVES.index(j))
            if i < 3:
                col = dot_t(s[hi:W, 2 * W + lo:2 * W + hi], w)
                s[hi:W, :] = s[hi:W, :] - dot(col, r)
            s[lo:hi, :] = r
            hook(j)


def split(a):
    high = a.astype(jnp.bfloat16)
    return high, (a - high.astype(F)).astype(jnp.bfloat16)


def v_rows(c, p):
    return [jnp.concatenate([c.vbuf[4 * p + i, k] for i in range(4)], axis=0) for k in range(p + 1)]


def panel_rows(c, p, pr, rcat):
    parts = [dot_t(tiles(c.rbuf.at[k]), v) for k, v in enumerate(v_rows(c, p))]
    own = parts[0] if p == 0 else parts[0] + parts[1]
    pr[p] = own

    @pl.when(c.row < 2)
    def _():
        place = lax.broadcasted_iota(jnp.int32, (W, W), 0) + c.row * W
        keep = place >= lax.broadcasted_iota(jnp.int32, (W, W), 1) + p * W
        pr[p, 0:W] = jnp.where(keep, pr[p, 0:W], 0.0)

    high, low = split(pr[p])
    rcat[:, p * W:(p + 1) * W] = high
    rcat[:, (2 + p) * W:(3 + p) * W] = high
    rcat[:, (4 + p) * W:(5 + p) * W] = low


def panel_columns(c, p, ccat):
    vs = v_rows(c, p)
    for ct in range(2):
        for pair in range(2):
            lanes = [ct * 4 + 2 * pair, ct * 4 + 2 * pair + 1]
            total = None
            for k, v in enumerate(vs):
                a = jnp.concatenate(
                    [c.cbuf[k, :, :, pl.ds(t, 8, stride=8), :].reshape(W, 128) for t in lanes], axis=1
                )
                part = dot(v, a)
                total = part if total is None else total + part
            if pair == 0:
                place = lax.broadcasted_iota(jnp.int32, (W, 2 * 128), 1)
                place = jnp.where(place < 128, place + ct * 128 + c.col * W, 2 * W)
                keep = place >= lax.broadcasted_iota(jnp.int32, (W, 2 * 128), 0) + p * W
                total = jnp.where(keep, total, 0.0)
            high, low = split(total)
            at = slice(lanes[0] * 128, lanes[0] * 128 + 256)
            ccat[p * W:(p + 1) * W, at] = high
            ccat[(2 + p) * W:(3 + p) * W, at] = low
            ccat[(4 + p) * W:(5 + p) * W, at] = high


def update(c, out, pr, rcat, ccat):
    step = 128
    for part in range(4):
        rows = slice(part * step, part * step + step)
        for pair in range(4):
            product = jnp.dot(rcat[rows, :], ccat[:, pair * 256:pair * 256 + 256], preferred_element_type=F)
            for half in range(2):
                at = (pl.ds(part * step * 8 + pair * 2 + half, step, stride=8), slice(None))
                c.hv[at] = c.hv[at] - product[:, half * 128:half * 128 + 128]
        whole = pl.ds(part * step * 8, step * 8)
        if part < 2:
            @pl.when(c.row < 2)
            def _():
                c.hv[whole, :] = jnp.zeros((step * 8, 128), F)
        for p in range(2):
            @pl.when(c.col == p)
            def _(p=p):
                for ct in range(2):
                    c.hv[pl.ds(part * step * 8 + ct * 4, step, stride=8), :] = pr[p, rows, ct * 128:ct * 128 + 128]
        pltpu.make_async_copy(c.hv.at[whole], out.at[whole], c.sems["local"].at[part]).start()
    for part in range(4):
        whole = pl.ds(part * step * 8, step * 8)
        pltpu.make_async_copy(c.hv.at[whole], out.at[whole], c.sems["local"].at[part]).wait()


def kernel(dims, h, out, hv, rsrc, cbuf, rbuf, vbuf, dbuf, via, s, pr, rcat, ccat, *sems):
    c = Comm(*dims, h, hv, rsrc, cbuf, rbuf, vbuf, dbuf, via, dict(zip(NAMES, sems)))
    load = pltpu.make_async_copy(h, hv, c.sems["local"].at[3])
    load.start()
    c.signal()
    load.wait()
    c.prepare()

    def begin():
        c.barrier()
        c.d_send()
        c.scatter_c()
        c.scatter_r()
        c.hand_on()

    slots = c.slots()

    @pl.when(c.root)
    def _():
        def hook(j):
            for t in ROOT.get(j, ()):
                c.slot(t)
        factor(c, s, begin, hook)
        for t in range(3, slots):
            c.slot(t)

    @pl.when(jnp.logical_not(c.root))
    def _():
        begin()
        for t in range(slots):
            c.slot(t)
            for depth in (1, 2, 3):
                for b in range(4):
                    if RELAY[depth][b] == t:
                        pl.when(c.depth(depth, b))(lambda b=b: c.v_relay(b))
            for b in range(4):
                if RELAY[4][b] == t:
                    c.v_collect(b)
    c.v_wait(0)
    panel_rows(c, 0, pr, rcat)
    panel_columns(c, 0, ccat)
    pl.when(jnp.logical_not(c.root))(lambda: c.v_collect(3))
    for b in range(1, 4):
        c.v_wait(b)
    panel_rows(c, 1, pr, rcat)
    panel_columns(c, 1, ccat)
    update(c, out, pr, rcat, ccat)
    c.finish()


def on_device(dims, hessian):
    i, r, l, w = hessian.shape
    nx, ny, nz = dims
    n = nx * ny
    flat = hessian.reshape(i, r, l, 2, 128).transpose(0, 1, 3, 2, 4).reshape(i * r * 2 * l, 128)
    out = pl.pallas_call(
        functools.partial(kernel, dims),
        out_shape=jax.ShapeDtypeStruct(flat.shape, F),
        in_specs=[pl.BlockSpec(memory_space=pltpu.HBM)],
        out_specs=pl.BlockSpec(memory_space=pl.ANY),
        scratch_shapes=[
            pltpu.VMEM(flat.shape, F),
            pltpu.VMEM((nz, 2, 2 * W // nz, 128), F),
            pltpu.VMEM((2, nx, ny, W * 8 // n, 128), F),
            pltpu.VMEM((2, nz, 2, 2 * W // nz, 128), F),
            pltpu.VMEM((8, 2, 64, W), F),
            pltpu.VMEM((2, 4, 2, 64, 128), F),
            pltpu.VMEM((ny, W * 8 // n // SUB, 128), F),
            pltpu.VMEM((W, 3 * W), F),
            pltpu.VMEM((2, 2 * W, W), F),
            pltpu.VMEM((2 * W, 6 * W), jnp.bfloat16),
            pltpu.VMEM((6 * W, 4 * W), jnp.bfloat16),
        ] + semaphores(nx, ny, nz),
        compiler_params=pltpu.CompilerParams(collective_id=0, has_side_effects=True, vmem_limit_bytes=40 << 20),
        name="panels",
    )(flat)
    return out.reshape(i, r, 2, l, 128).transpose(0, 1, 3, 2, 4).reshape(i, r, l, w)


def solution(mesh):
    spec = P(None, "row", None, "col")
    return jax.shard_map(
        functools.partial(on_device, (4, 8, 8)), mesh=mesh, in_specs=(spec,), out_specs=spec, check_vma=False
    )
```
